256 devices in a mesh: rows: 16 (over z_lo, y), out: 16 (over z_hi, x, core).
Axes of the slice: x: 4, y: 4, z: 8 (z_hi: 2, z_lo: 4; z = z_hi * 4 + z_lo), core: 2. Of those that a mesh axis runs over, the one named last changes fastest.
Arguments:
- predictions: bfloat16 [131072, 4096], P('rows', 'out'), may hold values from -5 to 5
- targets: bfloat16 [131072, 4096], P('rows', 'out'), may hold values from -4.5 to 4.5
- row_weight: bfloat16 [131072], P('rows'), may hold values from 0.25 to 4
- features: int32 [131072, 256], P('rows', 'out'), may hold values from 0 to 255
- leaf: int32 [131072], P('rows'), may hold values from 0 to 63
- sketch_matrix: bfloat16 [4096, 32], P('out'), may hold values from -0.00390625 to 0.00390625
Outputs:
- hist_grad: float32 [256, 256, 32], P('rows', 'out')
- hist_hess: float32 [256, 256], P('rows', 'out')
- leaf_values: float32 [64, 4096], P('rows', 'out')
The draws below stay inside these ranges and needn't reach their ends.
All inputs are finite; a program needn't handle non-finite values.
Results may differ from the reference program's by a relative error of at most 0.0022.
Values may be sent and summed in bfloat16 or wider, within the bound.
No kernel may reach another device: no remote copies, remote signals or barrier semaphores. Data moves between devices by JAX's collectives and lax.ppermute only.
A program may use at most 64 MiB of HBM per device.

```python
import math
import jax
import jax.numpy as jnp
from jax import lax

G = 4096
NF = 256
BINS = 256
K = 32
LEAVES = 64
CELLS = 131072


def leaf_rows(key):
    return jax.random.randint(jax.random.fold_in(key, 17), (CELLS,), 0, LEAVES)


def draw_leaf(key, part):
    chosen = leaf_rows(key)
    return chosen


def draw_targets(key, part):
    chosen = leaf_rows(key)
    key = jax.random.fold_in(key, 5)
    first_key, second_key = jax.random.split(key)
    offsets = jnp.clip(jax.random.normal(first_key, (LEAVES, G), jnp.float32), -3.0, 3.0)
    noise = jnp.clip(0.5 * jax.random.normal(second_key, (CELLS, G), jnp.float32), -1.5, 1.5)
    return (jnp.take(offsets, chosen, axis=0) + noise).astype(jnp.bfloat16)


def with_ends(result, stream_key, low, top_value):
    extent = result.shape
    spot = [jax.random.randint(jax.random.fold_in(stream_key, axis), (), 0, extent[axis]) for axis in range(len(extent))]
    result = result.at[tuple(spot)].set(low)
    longest = extent.index(max(extent))
    spot[longest] = (spot[longest] + 1) % extent[longest]
    return result.at[tuple(spot)].set(top_value)


def levels(rng, extent, cuts, low, top_value):
    gain, own = 1.0, jax.random.fold_in(rng, 6)
    for dim, blocks in cuts:
        steps = jnp.exp(jax.random.uniform(jax.random.fold_in(own, dim), (blocks,), jnp.float32, low / len(cuts), top_value / len(cuts)))
        gain = gain * jnp.repeat(steps, extent[dim] // blocks).reshape([-1 if axis == dim else 1 for axis in range(len(extent))])
    return gain


def gaussian(key, dims, deviation, limit, pieces=(), kind=jnp.bfloat16):
    factor_of = levels(key, dims, pieces, -0.22, 0.18) if pieces else 1.0
    entries = jax.random.normal(key, dims, jnp.float32) * deviation * factor_of
    return jnp.minimum(jnp.maximum(entries, -limit), limit).astype(kind)


def setup_inputs(seed: int = 0) -> dict:
    splits = jax.random.split(jax.random.key(seed), 7)
    return {
        "predictions": gaussian(splits[0], (CELLS, G), 1.0, 5.0, ((0, 16), (1, 16))),
        "targets": draw_targets(jax.random.fold_in(splits[6], 71), 0),
        "row_weight": jnp.clip(jnp.exp(math.log(4.0) - 2.7725887 * jax.random.uniform(splits[2], (CELLS,), jnp.float32) ** levels(splits[2], (CELLS,), ((0, 16),), -0.2, 0.2)), 0.25, 4.0).astype(jnp.bfloat16),
        "features": with_ends(jax.random.randint(splits[3], (CELLS, NF), 0, BINS), jax.random.fold_in(splits[3], 1), 0, BINS - 1).astype(jnp.int32),
        "leaf": draw_leaf(jax.random.fold_in(splits[6], 71), 0),
        "sketch_matrix": gaussian(splits[5], (G, K), (G * CELLS // BINS) ** -0.5, 0.00390625, ((0, 16),)),
    }


ridge = 1.0


def reference(predictions, targets, row_weight, features, leaf, sketch_matrix):
    weight_wide = row_weight.astype(jnp.float32)
    gradient = (weight_wide[:, None] * (predictions.astype(jnp.float32) - targets.astype(jnp.float32))).astype(jnp.bfloat16)
    sketch = jnp.dot(gradient, sketch_matrix, preferred_element_type=jnp.float32).astype(jnp.bfloat16)
    augmented = jnp.concatenate([sketch.astype(jnp.float32), weight_wide[:, None]], axis=1)
    group = 16
    columns = augmented.shape[1]

    def feature_block(first):
        chosen = lax.dynamic_slice_in_dim(features, first, group, 1)
        bin_ids = chosen + BINS * jnp.arange(group, dtype=jnp.int32)[None, :]
        spread = jnp.broadcast_to(augmented[:, None, :], (augmented.shape[0], group, columns))
        summed = jax.ops.segment_sum(spread.reshape(-1, columns), bin_ids.reshape(-1), num_segments=group * BINS)
        return summed.reshape(group, BINS, columns)

    starts = jnp.arange(0, NF, group, dtype=jnp.int32)
    blocks = lax.map(feature_block, starts).reshape(NF, BINS, columns)
    histogram = jnp.transpose(blocks, (1, 0, 2))
    hist_grad = histogram[:, :, :K]
    hist_hess = histogram[:, :, K] / (CELLS / BINS)
    leaf_sums = jax.ops.segment_sum(gradient.astype(jnp.float32), leaf, num_segments=LEAVES)
    leaf_weights = jax.ops.segment_sum(weight_wide, leaf, num_segments=LEAVES)
    leaf_values = -leaf_sums / (leaf_weights[:, None] + ridge)
    return hist_grad, hist_hess, leaf_values
```

```python
import functools

import jax
import jax.numpy as jnp
from jax import lax
from jax.experimental import pallas as pl
from jax.experimental.pallas import tpu as pltpu
from jax.sharding import PartitionSpec as P

BINS = 256
LEAVES = 64
RIDGE = 1.0
F32 = jnp.float32
BF16 = jnp.bfloat16
BLOCK = 1024
CONTRACT_LAST = (((1,), (1,)), ((), ()))


def gradient_kernel(where, pred, targ, weight, leaf, matrix_t, leaf_in, sketch_out, leaf_out, sums, weights, *, steps):
    step = pl.program_id(0)
    cells = pred.shape[0]

    @pl.when(step == 0)
    def _():
        sums[...] = jnp.zeros_like(sums)
        weights[...] = jnp.zeros_like(weights)

    w_row = weight[...]
    w_wide = w_row.astype(F32)
    w_tile = jnp.concatenate([w_wide[:, 128 * s : 128 * s + 128] for s in range(cells // 128)], axis=0)
    w_cols = jnp.transpose(w_tile)
    pieces = []
    for s in range(cells // 128):
        rows = slice(128 * s, 128 * s + 128)
        diff = pred[rows, :].astype(F32) - targ[rows, :].astype(F32)
        pieces.append((w_cols[:, s : s + 1] * diff).astype(BF16))
    gradient = jnp.concatenate(pieces, axis=0)
    sketch_out[...] = lax.dot_general(matrix_t[...], gradient, CONTRACT_LAST, preferred_element_type=F32)
    own = leaf[...] ^ where[2]
    place = ((own >> 2) & 3) * 16 + (own >> 4) * 4 + (own & 3)
    onehot = jnp.where(lax.broadcasted_iota(jnp.int32, (LEAVES, cells), 0) == place, 1.0, 0.0).astype(BF16)
    sums[...] += jnp.dot(onehot, gradient, preferred_element_type=F32)
    weights[...] += lax.dot_general(
        onehot, jnp.broadcast_to(w_row, (128, cells)), CONTRACT_LAST, preferred_element_type=F32
    )

    @pl.when(step == steps - 1)
    def _():
        for y in range(4):
            for z in range(4):
                top = 16 * y + 4 * z
                for h in range(2):
                    at = 8 * z + 4 * h
                    leaf_out[y, at : at + 4, :] = (
                        leaf_in[y, at : at + 4, :] + sums[top : top + 4, 128 * h : 128 * h + 128]
                    )
                    leaf_out[y, 32 + at : 36 + at, :] = leaf_in[y, 32 + at : 36 + at, :] + weights[top : top + 4, :]


def gradient_half(where, pred, targ, weight, leaf, matrix_t, leaf_in, first):
    genes = pred.shape[1]
    steps = pred.shape[0] // BLOCK // 2
    block = lambda j, where: (j + first) ^ where[0]
    return pl.pallas_call(
        functools.partial(gradient_kernel, steps=steps),
        grid_spec=pltpu.PrefetchScalarGridSpec(
            num_scalar_prefetch=1,
            grid=(steps,),
            in_specs=[
                pl.BlockSpec((BLOCK, genes), lambda j, s: (block(j, s), 0)),
                pl.BlockSpec((BLOCK, genes), lambda j, s: (block(j, s), 0)),
                pl.BlockSpec((1, BLOCK), lambda j, s: (0, block(j, s))),
                pl.BlockSpec((1, BLOCK), lambda j, s: (0, block(j, s))),
                pl.BlockSpec(matrix_t.shape, lambda j, s: (0, 0)),
                pl.BlockSpec((4, 64, 128), lambda j, s: (0, 0, 0)),
            ],
            out_specs=[
                pl.BlockSpec((matrix_t.shape[0], BLOCK), lambda j, s: (0, j)),
                pl.BlockSpec((4, 64, 128), lambda j, s: (0, 0, 0)),
            ],
            scratch_shapes=[pltpu.VMEM((LEAVES, genes), F32), pltpu.VMEM((LEAVES, 128), F32)],
        ),
        out_shape=[
            jax.ShapeDtypeStruct((matrix_t.shape[0], steps * BLOCK), F32),
            jax.ShapeDtypeStruct((4, 64, 128), F32),
        ],
        compiler_params=pltpu.CompilerParams(vmem_limit_bytes=40 * 1024 * 1024),
        cost_estimate=pl.CostEstimate(flops=2 * 4096 * 256 * 300, bytes_accessed=5000000, transcendentals=0),
        name="gradient",
    )(where, pred, targ, weight, leaf, matrix_t, leaf_in)


def histogram_kernel(where, feat, sketch, weight, leaf_part, o0, o1, o2, o3, hess, *, steps):
    step = pl.program_id(0)
    outs = (o0, o1, o2, o3)
    cells = feat.shape[1]

    @pl.when(step == 0)
    def _():
        hess[...] = jnp.zeros_like(hess)
        for y in range(4):
            outs[y][0:256, :] = jnp.zeros((256, 128), F32)
            outs[y][272:336, :] = leaf_part[y]

    sketch_all = sketch[...]
    w_all = jnp.broadcast_to(weight[...], (16, cells))
    rows64 = lax.broadcasted_iota(jnp.int32, (64, cells), 0).astype(BF16)
    rows16 = lax.broadcasted_iota(jnp.int32, (16, cells), 0).astype(BF16)
    zero = jnp.zeros((), BF16)
    one = jnp.ones((), BF16)
    for f in range(16):
        own = feat[f : f + 1, :] ^ where[1]
        low = (own & 63).astype(F32).astype(BF16)
        high = own >> 6
        group = jnp.broadcast_to(high.astype(F32).astype(BF16), (32, cells))
        left = jnp.where(rows64 == low, one, zero)
        parts = [jnp.where(group == jnp.asarray(z, BF16), sketch_all, zero) for z in range(4)]
        spot = (high * 4 + (f % 4)).astype(F32).astype(BF16)
        parts.append(jnp.where(rows16 == spot, w_all, zero))
        right = jnp.concatenate(parts, axis=0)
        both = lax.dot_general(left, right, CONTRACT_LAST, preferred_element_type=F32)
        for y in range(4):
            outs[y][16 * f : 16 * f + 16, :] += both[16 * y : 16 * y + 16, :128]
        hess[f // 4] += both[:, 128:144]

    @pl.when(step == steps - 1)
    def _():
        held = [hess[g] for g in range(4)]
        lanes = [held[g][:, 4 * z : 4 * z + 4] for z in range(4) for g in range(4)]
        whole = jnp.concatenate(lanes + [jnp.zeros((64, 64), F32)], axis=1)
        for y in range(4):
            outs[y][256:272, :] = whole[16 * y : 16 * y + 16, :]


def histogram(where, feat_t, sketch, weight, leaf_part):
    cells = feat_t.shape[1]
    steps = cells // BLOCK
    return pl.pallas_call(
        functools.partial(histogram_kernel, steps=steps),
        grid_spec=pltpu.PrefetchScalarGridSpec(
            num_scalar_prefetch=1,
            grid=(steps,),
            in_specs=[
                pl.BlockSpec((16, BLOCK), lambda j, s: (0, j ^ s[0])),
                pl.BlockSpec((32, BLOCK), lambda j, s: (0, j)),
                pl.BlockSpec((1, BLOCK), lambda j, s: (0, j ^ s[0])),
                pl.BlockSpec((4, 64, 128), lambda j, s: (0, 0, 0)),
            ],
            out_specs=[pl.BlockSpec((336, 128), lambda j, s: (0, 0))] * 4,
            scratch_shapes=[pltpu.VMEM((4, 64, 16), F32)],
        ),
        out_shape=[jax.ShapeDtypeStruct((336, 128), F32)] * 4,
        compiler_params=pltpu.CompilerParams(vmem_limit_bytes=40 * 1024 * 1024),
        cost_estimate=pl.CostEstimate(flops=2 * 8192 * 4096 * 256, bytes_accessed=1500000, transcendentals=0),
        name="histogram",
    )(where, feat_t, sketch, weight, leaf_part)


def regroup_kernel(a, b, c, d, o0, o1, o2, o3):
    outs = (o0, o1, o2, o3)
    total = a[...] + b[...] + c[...] + d[...]
    for z in range(4):
        outs[z][0:64, :] = jnp.concatenate(
            [total[64 * q : 64 * q + 64, 32 * z : 32 * z + 32] for q in range(4)], axis=1
        )
        outs[z][64:80, :] = jnp.concatenate(
            [total[256:272, 16 * z : 16 * z + 16], jnp.zeros((16, 112), F32)], axis=1
        )
        outs[z][80:88, :] = total[272 + 8 * z : 280 + 8 * z, :]
        outs[z][88:96, :] = total[304 + 8 * z : 312 + 8 * z, :]


def regroup(a, b, c, d):
    return pl.pallas_call(
        regroup_kernel,
        out_shape=[jax.ShapeDtypeStruct((96, 128), F32)] * 4,
        name="regroup",
    )(a, b, c, d)


def finish_kernel(a, b, c, d, grad_out, hess_out, leaf_out, rows, *, per_bin):
    total = a[...] + b[...] + c[...] + d[...]
    for q in range(4):
        rows[64 * q : 64 * q + 64, 0:32] = total[0:64, 32 * q : 32 * q + 32]
    for i in range(16):
        grad_out[i] = rows[pl.ds(i, 16, stride=16), :][:, 0:32]
    hess_out[...] = total[64:80, 0:16] / per_bin
    values = -total[80:88, :] / (total[88:96, :] + RIDGE)
    leaf_out[:, 0:128] = values[0:4]
    leaf_out[:, 128:256] = values[4:8]


def finish(a, b, c, d, per_bin):
    return pl.pallas_call(
        functools.partial(finish_kernel, per_bin=per_bin),
        out_shape=[
            jax.ShapeDtypeStruct((16, 16, 32), F32),
            jax.ShapeDtypeStruct((16, 16), F32),
            jax.ShapeDtypeStruct((4, 256), F32),
        ],
        scratch_shapes=[pltpu.VMEM((256, 128), F32)],
        name="finish",
    )(a, b, c, d)


def swap(value, axis, flip):
    return lax.ppermute(value, axis, [(i, i ^ flip) for i in range(16)])


def per_device(predictions, targets, row_weight, features, leaf, sketch_matrix):
    out_at = lax.axis_index("out")
    rows_at = lax.axis_index("rows")
    where = jnp.stack([(out_at & 1) * 4 + ((out_at >> 1) & 3), rows_at * 16, rows_at * 4]).astype(jnp.int32)
    cells = predictions.shape[0]
    weight = row_weight.reshape(1, cells)
    leaf_row = leaf.reshape(1, cells)
    matrix_t = sketch_matrix.T
    args = (where, predictions, targets, weight, leaf_row, matrix_t)
    other, leaf_part = gradient_half(*args, jnp.zeros((4, 64, 128), F32), 4)
    arrived = swap(other, "out", 1)
    mine, leaf_part = gradient_half(*args, leaf_part, 0)
    chip = mine + arrived
    blocks = [chip[:, BLOCK * j : BLOCK * (j + 1)] for j in range(4)]
    far = [swap(blocks[j], "out", 2 * j) for j in (2, 1, 3)]
    part = blocks[0] + far[0] + far[1] + far[2]
    own = (part + swap(part, "out", 8)).astype(BF16)
    sketch = jnp.concatenate([own] + [swap(own, "out", 2 * j) for j in (1, 2, 3)], axis=1)
    sketch = jnp.concatenate([sketch, swap(sketch, "out", 1)], axis=1)
    slices = histogram(where, features.T, sketch, weight, leaf_part)
    slices = regroup(slices[0], *[swap(slices[j], "rows", j) for j in (1, 2, 3)])
    return tuple(
        finish(slices[0], *[swap(slices[j], "rows", 4 * j) for j in (1, 2, 3)], float(cells * 16 // BINS))
    )


def solution(mesh):
    return jax.shard_map(
        per_device,
        mesh=mesh,
        in_specs=(
            P("rows", "out"),
            P("rows", "out"),
            P("rows"),
            P("rows", "out"),
            P("rows"),
            P("out", None),
        ),
        out_specs=(P("rows", "out", None), P("rows", "out"), P("rows", "out")),
        check_vma=False,
    )
```

```python
import functools

import jax
import jax.numpy as jnp
from jax import lax
from jax.experimental import pallas as pl
from jax.experimental.pallas import tpu as pltpu
from jax.sharding import PartitionSpec as P

BINS = 256
LEAVES = 64
RIDGE = 1.0
F32 = jnp.float32
BF16 = jnp.bfloat16
BLOCK = 1024
CONTRACT_LAST = (((1,), (1,)), ((), ()))


def own_block():
    out_at = lax.axis_index("out")
    return (out_at & 1) * 4 + ((out_at >> 1) & 3)


def lanes_of(block):
    return pl.ds(pl.multiple_of(block * BLOCK, BLOCK), BLOCK)


def gradient_kernel(*refs, first, parts):
    pred, targ, weight, leaf, matrix_t = refs[:5]
    leaf_in = refs[5] if len(refs) == 13 else None
    sketch_out, leaf_out, pred_here, targ_here, sums, weights = refs[-7:-1]
    arrived = refs[-1]
    me = own_block()
    leaf_flip = lax.axis_index("rows") * 4
    size = BLOCK // parts
    copies = []
    for j in range(4):
        for part in range(parts):
            n = j * parts + part
            rows = pl.ds(pl.multiple_of(((j + first) ^ me) * BLOCK + part * size, size), size)
            pair = [
                pltpu.make_async_copy(pred.at[rows, :], pred_here.at[n], arrived.at[0, n]),
                pltpu.make_async_copy(targ.at[rows, :], targ_here.at[n], arrived.at[1, n]),
            ]
            for copy in pair:
                copy.start()
            copies.append(pair)
    for j in range(4):
        w_wide = weight[:, lanes_of((j + first) ^ me)]
        own = leaf[:, lanes_of((j + first) ^ me)] ^ leaf_flip
        place = ((own >> 2) & 3) * 16 + (own >> 4) * 4 + (own & 3)
        onehot = jnp.where(lax.broadcasted_iota(jnp.int32, (LEAVES, BLOCK), 0) == place, 1.0, 0.0).astype(BF16)
        w_cols = jnp.transpose(
            jnp.concatenate([w_wide[:, 128 * s : 128 * s + 128] for s in range(BLOCK // 128)], axis=0)
        )
        added = None
        for part in range(parts):
            n = j * parts + part
            for copy in copies[n]:
                copy.wait()
            pieces = []
            for s in range(size // 128):
                rows = slice(128 * s, 128 * s + 128)
                diff = pred_here[n, rows, :].astype(F32) - targ_here[n, rows, :].astype(F32)
                at = part * (size // 128) + s
                pieces.append((w_cols[:, at : at + 1] * diff).astype(BF16))
            gradient = jnp.concatenate(pieces, axis=0)
            sketch_out[:, n * size : n * size + size] = lax.dot_general(
                matrix_t[...], gradient, CONTRACT_LAST, preferred_element_type=F32
            )
            piece = jnp.dot(onehot[:, part * size : part * size + size], gradient, preferred_element_type=F32)
            added = piece if added is None else added + piece
        w_rows = jnp.broadcast_to(w_wide.astype(BF16), (16, BLOCK))
        w_added = lax.dot_general(onehot, w_rows, CONTRACT_LAST, preferred_element_type=F32)
        if j == 0:
            sums[...] = added
            weights[...] = w_added
        else:
            sums[...] += added
            weights[...] += w_added
    for y in range(4):
        for z in range(4):
            top = 16 * y + 4 * z
            pieces = [sums[top : top + 4, 0:128], sums[top : top + 4, 128:256]]
            pieces += [jnp.broadcast_to(weights[top : top + 4, 0:1], (4, 128))] * 2
            for value, at in zip(pieces, (8 * z, 8 * z + 4, 32 + 8 * z, 36 + 8 * z)):
                leaf_out[y, at : at + 4, :] = value if leaf_in is None else value + leaf_in[y, at : at + 4, :]


def gradient_half(pred, targ, weight, leaf, matrix_t, leaf_in, first):
    genes = pred.shape[1]
    half = pred.shape[0] // 2
    parts = 2
    given = [pred, targ, weight, leaf, matrix_t] + ([] if leaf_in is None else [leaf_in])
    whole = pl.BlockSpec(memory_space=pltpu.VMEM)
    return pl.pallas_call(
        functools.partial(gradient_kernel, first=first, parts=parts),
        in_specs=[pl.BlockSpec(memory_space=pltpu.HBM)] * 2 + [whole] * (len(given) - 2),
        out_specs=[whole, whole],
        scratch_shapes=[
            pltpu.VMEM((4 * parts, BLOCK // parts, genes), BF16),
            pltpu.VMEM((4 * parts, BLOCK // parts, genes), BF16),
            pltpu.VMEM((LEAVES, genes), F32),
            pltpu.VMEM((LEAVES, 16), F32),
            pltpu.SemaphoreType.DMA((2, 4 * parts)),
        ],
        out_shape=[
            jax.ShapeDtypeStruct((matrix_t.shape[0], half), F32),
            jax.ShapeDtypeStruct((4, 64, 128), F32),
        ],
        compiler_params=pltpu.CompilerParams(vmem_limit_bytes=61 * 1024 * 1024),
        cost_estimate=pl.CostEstimate(flops=2 * half * 256 * 300, bytes_accessed=5000000, transcendentals=0),
        name="gradient",
    )(*given)


def histogram_kernel(feat, sketch, weight, leaf_part, o0, o1, o2, o3, held, hess, *, steps):
    step = pl.program_id(0)
    outs = (o0, o1, o2, o3)
    wide = sketch.shape[1]
    blocks = wide // BLOCK
    me = own_block()
    bin_flip = lax.axis_index("rows") * 16

    @pl.when(step == 0)
    def _():
        held[...] = jnp.zeros_like(held)
        hess[...] = jnp.zeros_like(hess)

    places = [lanes_of((step * blocks + b) ^ me) for b in range(blocks)]
    sketch_all = sketch[...]
    w_row = jnp.concatenate([weight[:, place] for place in places], axis=1)
    w_all = jnp.broadcast_to(w_row.astype(BF16), (16, wide))
    rows128 = lax.broadcasted_iota(jnp.int32, (128, wide), 0).astype(BF16)
    rows16 = lax.broadcasted_iota(jnp.int32, (16, wide), 0).astype(BF16)
    zero = jnp.zeros((), BF16)
    one = jnp.ones((), BF16)
    for f in range(16):
        own = jnp.concatenate([feat[f : f + 1, place] for place in places], axis=1) ^ bin_flip
        low = (own & 127).astype(F32).astype(BF16)
        top = own >> 7
        group = jnp.broadcast_to(top.astype(F32).astype(BF16), (32, wide))
        left = jnp.where(rows128 == low, one, zero)
        spot = (top * 8 + (f % 8)).astype(F32).astype(BF16)
        right = jnp.concatenate(
            [
                jnp.where(group == zero, sketch_all, zero),
                jnp.where(group == zero, zero, sketch_all),
                jnp.where(rows16 == spot, w_all, zero),
            ],
            axis=0,
        )
        both = lax.dot_general(left, right, CONTRACT_LAST, preferred_element_type=F32)
        held[f] += both[:, 0:64]
        hess[f // 8] += both[:, 64:80]

    @pl.when(step == steps - 1)
    def _():
        for y in range(4):
            near, far = slice(16 * y, 16 * y + 16), slice(64 + 16 * y, 80 + 16 * y)
            for f in range(16):
                outs[y][16 * f : 16 * f + 16, :] = jnp.concatenate([held[f, near, :], held[f, far, :]], axis=1)
            lanes = [
                hess[g, (far if z & 1 else near), 8 * (z >> 1) : 8 * (z >> 1) + 8] for z in range(4) for g in range(2)
            ]
            outs[y][256:272, :] = jnp.concatenate(lanes + [jnp.zeros((16, 64), F32)], axis=1)
            outs[y][272:336, :] = leaf_part[y]


def histogram(feat_t, sketch, weight, leaf_part):
    cells = feat_t.shape[1]
    wide = 2 * BLOCK
    steps = cells // wide
    whole = pl.BlockSpec(memory_space=pltpu.VMEM)
    return pl.pallas_call(
        functools.partial(histogram_kernel, steps=steps),
        grid=(steps,),
        in_specs=[whole, pl.BlockSpec((32, wide), lambda j: (0, j)), whole, whole],
        out_specs=[whole] * 4,
        scratch_shapes=[pltpu.VMEM((16, 128, 64), F32), pltpu.VMEM((2, 128, 16), F32)],
        out_shape=[jax.ShapeDtypeStruct((336, 128), F32)] * 4,
        compiler_params=pltpu.CompilerParams(vmem_limit_bytes=24 * 1024 * 1024),
        cost_estimate=pl.CostEstimate(flops=2 * 8192 * 4096 * 256, bytes_accessed=1500000, transcendentals=0),
        name="histogram",
    )(feat_t, sketch, weight, leaf_part)


def regroup_kernel(a, b, c, d, o0, o1, o2, o3):
    outs = (o0, o1, o2, o3)
    total = a[...] + b[...] + c[...] + d[...]
    for z in range(4):
        lane = 64 * (z & 1) + 32 * (z >> 1)
        outs[z][0:64, :] = jnp.concatenate(
            [total[64 * q : 64 * q + 64, lane : lane + 32] for q in range(4)], axis=1
        )
        outs[z][64:80, :] = jnp.concatenate(
            [total[256:272, 16 * z : 16 * z + 16], jnp.zeros((16, 112), F32)], axis=1
        )
        outs[z][80:88, :] = total[272 + 8 * z : 280 + 8 * z, :]
        outs[z][88:96, :] = total[304 + 8 * z : 312 + 8 * z, :]


def regroup(a, b, c, d):
    return pl.pallas_call(
        regroup_kernel,
        out_shape=[jax.ShapeDtypeStruct((96, 128), F32)] * 4,
        compiler_params=pltpu.CompilerParams(vmem_limit_bytes=8 * 1024 * 1024),
        name="regroup",
    )(a, b, c, d)


def finish_kernel(a, b, c, d, grad_out, hess_out, leaf_out, rows, *, per_bin):
    total = a[...] + b[...] + c[...] + d[...]
    for q in range(4):
        rows[64 * q : 64 * q + 64, 0:32] = total[0:64, 32 * q : 32 * q + 32]
    for i in range(16):
        grad_out[i] = rows[pl.ds(i, 16, stride=16), :][:, 0:32]
    hess_out[...] = total[64:80, 0:16] / per_bin
    values = -total[80:88, :] / (total[88:96, :] + RIDGE)
    leaf_out[:, 0:128] = values[0:4]
    leaf_out[:, 128:256] = values[4:8]


def finish(a, b, c, d, per_bin):
    return pl.pallas_call(
        functools.partial(finish_kernel, per_bin=per_bin),
        out_shape=[
            jax.ShapeDtypeStruct((16, 16, 32), F32),
            jax.ShapeDtypeStruct((16, 16), F32),
            jax.ShapeDtypeStruct((4, 256), F32),
        ],
        scratch_shapes=[pltpu.VMEM((256, 128), F32)],
        compiler_params=pltpu.CompilerParams(vmem_limit_bytes=8 * 1024 * 1024),
        name="finish",
    )(a, b, c, d)


def swap(value, axis, flip):
    return lax.ppermute(value, axis, [(i, i ^ flip) for i in range(16)])


def per_device(predictions, targets, row_weight, features, leaf, sketch_matrix):
    cells = predictions.shape[0]
    weight = row_weight.astype(F32).reshape(1, cells)
    args = (predictions, targets, weight, leaf.reshape(1, cells), sketch_matrix.T)
    other, leaf_part = gradient_half(*args, None, 4)
    arrived = swap(other, "out", 1)
    mine, leaf_part = gradient_half(*args, leaf_part, 0)
    chip = mine + arrived
    blocks = [chip[:, BLOCK * j : BLOCK * (j + 1)] for j in range(4)]
    far = [swap(blocks[j], "out", 2 * j) for j in (2, 1, 3)]
    part = blocks[0] + far[0] + far[1] + far[2]
    own = (part + swap(part, "out", 8)).astype(BF16)
    sketch = jnp.concatenate([own] + [swap(own, "out", 2 * j) for j in (1, 2, 3)], axis=1)
    sketch = jnp.concatenate([sketch, swap(sketch, "out", 1)], axis=1)
    slices = histogram(features.T, sketch, weight, leaf_part)
    slices = regroup(slices[0], *[swap(slices[j], "rows", j) for j in (1, 2, 3)])
    return tuple(
        finish(slices[0], *[swap(slices[j], "rows", 4 * j) for j in (1, 2, 3)], float(cells * 16 // BINS))
    )


def solution(mesh):
    return jax.shard_map(
        per_device,
        mesh=mesh,
        in_specs=(
            P("rows", "out"),
            P("rows", "out"),
            P("rows"),
            P("rows", "out"),
            P("rows"),
            P("out", None),
        ),
        out_specs=(P("rows", "out", None), P("rows", "out"), P("rows", "out")),
        check_vma=False,
    )
```

```python
import functools

import jax
import jax.numpy as jnp
from jax import lax
from jax.experimental import pallas as pl
from jax.experimental.pallas import tpu as pltpu
from jax.sharding import PartitionSpec as P

BINS = 256
LEAVES = 64
RIDGE = 1.0
F32 = jnp.float32
BF16 = jnp.bfloat16
BLOCK = 1024
CONTRACT_LAST = (((1,), (1,)), ((), ()))


def group_count(rows):
    return rows // 16


def encoded_rows(rows):
    return rows + -(-group_count(rows) // 16) * 16


def encode_into(out, value):
    rows = value.shape[0]
    count = group_count(rows)
    padded = encoded_rows(rows) - rows
    tops = [jnp.max(jnp.abs(value[16 * g : 16 * g + 16, :]), axis=0, keepdims=True) for g in range(count)]
    tops.append(jnp.zeros((padded - count, 128), F32))
    exponent = jnp.ceil(jnp.log2(jnp.maximum(jnp.concatenate(tops, axis=0), 1e-30)))
    scale = jnp.exp2(14.0 - exponent)
    for g in range(count):
        scaled = value[16 * g : 16 * g + 16, :] * scale[g : g + 1, :]
        out[16 * g : 16 * g + 16, :] = jnp.round(scaled).astype(jnp.int32).astype(jnp.int16)
    out[rows : rows + padded, :] = exponent.astype(jnp.int32).astype(jnp.int16)


def decode(code, rows):
    count = group_count(rows)
    whole = code[...].astype(jnp.int32).astype(F32)
    scale = jnp.exp2(whole[rows:, :] - 14.0)
    return jnp.concatenate([whole[16 * g : 16 * g + 16, :] * scale[g : g + 1, :] for g in range(count)], axis=0)


def own_block():
    out_at = lax.axis_index("out")
    return (out_at & 1) * 4 + ((out_at >> 1) & 3)


def lanes_of(block):
    return pl.ds(pl.multiple_of(block * BLOCK, BLOCK), BLOCK)


def gradient_kernel(*refs, first, parts):
    pred, targ, weight, leaf, matrix_t = refs[:5]
    leaf_in = refs[5] if len(refs) == 13 else None
    sketch_out, leaf_out, pred_here, targ_here, sums, weights = refs[-7:-1]
    arrived = refs[-1]
    me = own_block()
    leaf_flip = lax.axis_index("rows") * 4
    size = BLOCK // parts
    copies = []
    for j in range(4):
        for part in range(parts):
            n = j * parts + part
            rows = pl.ds(pl.multiple_of(((j + first) ^ me) * BLOCK + part * size, size), size)
            pair = [
                pltpu.make_async_copy(pred.at[rows, :], pred_here.at[n], arrived.at[0, n]),
                pltpu.make_async_copy(targ.at[rows, :], targ_here.at[n], arrived.at[1, n]),
            ]
            for copy in pair:
                copy.start()
            copies.append(pair)
    for j in range(4):
        w_wide = weight[:, lanes_of((j + first) ^ me)]
        own = leaf[:, lanes_of((j + first) ^ me)] ^ leaf_flip
        place = ((own >> 2) & 3) * 16 + (own >> 4) * 4 + (own & 3)
        onehot = jnp.where(lax.broadcasted_iota(jnp.int32, (LEAVES, BLOCK), 0) == place, 1.0, 0.0).astype(BF16)
        w_cols = jnp.transpose(
            jnp.concatenate([w_wide[:, 128 * s : 128 * s + 128] for s in range(BLOCK // 128)], axis=0)
        )
        added = None
        for part in range(parts):
            n = j * parts + part
            for copy in copies[n]:
                copy.wait()
            pieces = []
            for s in range(size // 128):
                rows = slice(128 * s, 128 * s + 128)
                diff = pred_here[n, rows, :].astype(F32) - targ_here[n, rows, :].astype(F32)
                at = part * (size // 128) + s
                pieces.append((w_cols[:, at : at + 1] * diff).astype(BF16))
            gradient = jnp.concatenate(pieces, axis=0)
            sketch_out[:, n * size : n * size + size] = lax.dot_general(
                matrix_t[...], gradient, CONTRACT_LAST, preferred_element_type=F32
            )
            piece = jnp.dot(onehot[:, part * size : part * size + size], gradient, preferred_element_type=F32)
            added = piece if added is None else added + piece
        w_rows = jnp.broadcast_to(w_wide.astype(BF16), (16, BLOCK))
        w_added = lax.dot_general(onehot, w_rows, CONTRACT_LAST, preferred_element_type=F32)
        if j == 0:
            sums[...] = added
            weights[...] = w_added
        else:
            sums[...] += added
            weights[...] += w_added
    for y in range(4):
        for z in range(4):
            top = 16 * y + 4 * z
            pieces = [sums[top : top + 4, 0:128], sums[top : top + 4, 128:256]]
            pieces += [jnp.broadcast_to(weights[top : top + 4, 0:1], (4, 128))] * 2
            for value, at in zip(pieces, (8 * z, 8 * z + 4, 32 + 8 * z, 36 + 8 * z)):
                leaf_out[y, at : at + 4, :] = value if leaf_in is None else value + leaf_in[y, at : at + 4, :]


def gradient_half(pred, targ, weight, leaf, matrix_t, leaf_in, first):
    genes = pred.shape[1]
    half = pred.shape[0] // 2
    parts = 2
    given = [pred, targ, weight, leaf, matrix_t] + ([] if leaf_in is None else [leaf_in])
    whole = pl.BlockSpec(memory_space=pltpu.VMEM)
    return pl.pallas_call(
        functools.partial(gradient_kernel, first=first, parts=parts),
        in_specs=[pl.BlockSpec(memory_space=pltpu.HBM)] * 2 + [whole] * (len(given) - 2),
        out_specs=[whole, whole],
        scratch_shapes=[
            pltpu.VMEM((4 * parts, BLOCK // parts, genes), BF16),
            pltpu.VMEM((4 * parts, BLOCK // parts, genes), BF16),
            pltpu.VMEM((LEAVES, genes), F32),
            pltpu.VMEM((LEAVES, 16), F32),
            pltpu.SemaphoreType.DMA((2, 4 * parts)),
        ],
        out_shape=[
            jax.ShapeDtypeStruct((matrix_t.shape[0], half), F32),
            jax.ShapeDtypeStruct((4, 64, 128), F32),
        ],
        compiler_params=pltpu.CompilerParams(vmem_limit_bytes=51 * 1024 * 1024),
        cost_estimate=pl.CostEstimate(flops=2 * half * 256 * 300, bytes_accessed=5000000, transcendentals=0),
        name="gradient",
    )(*given)


def histogram_kernel(feat, sketch, weight, leaf_part, o0, o1, o2, o3, held, hess, slab, *, steps):
    step = pl.program_id(0)
    codes = (o1, o2, o3)
    wide = sketch.shape[1]
    blocks = wide // BLOCK
    me = own_block()
    bin_flip = lax.axis_index("rows") * 16

    @pl.when(step == 0)
    def _():
        held[...] = jnp.zeros_like(held)
        hess[...] = jnp.zeros_like(hess)

    places = [lanes_of((step * blocks + b) ^ me) for b in range(blocks)]
    sketch_all = sketch[...]
    w_row = jnp.concatenate([weight[:, place] for place in places], axis=1)
    w_all = jnp.broadcast_to(w_row.astype(BF16), (16, wide))
    rows128 = lax.broadcasted_iota(jnp.int32, (128, wide), 0).astype(BF16)
    rows16 = lax.broadcasted_iota(jnp.int32, (16, wide), 0).astype(BF16)
    zero = jnp.zeros((), BF16)
    one = jnp.ones((), BF16)
    for f in range(16):
        own = jnp.concatenate([feat[f : f + 1, place] for place in places], axis=1) ^ bin_flip
        low = (own & 127).astype(F32).astype(BF16)
        top = own >> 7
        group = jnp.broadcast_to(top.astype(F32).astype(BF16), (32, wide))
        left = jnp.where(rows128 == low, one, zero)
        spot = (top * 8 + (f % 8)).astype(F32).astype(BF16)
        right = jnp.concatenate(
            [
                jnp.where(group == zero, sketch_all, zero),
                jnp.where(group == zero, zero, sketch_all),
                jnp.where(rows16 == spot, w_all, zero),
            ],
            axis=0,
        )
        both = lax.dot_general(left, right, CONTRACT_LAST, preferred_element_type=F32)
        held[f] += both[:, 0:64]
        hess[f // 8] += both[:, 64:80]

    @pl.when(step == steps - 1)
    def _():
        for y in range(4):
            near, far = slice(16 * y, 16 * y + 16), slice(64 + 16 * y, 80 + 16 * y)
            target = slab if y else o0
            for f in range(16):
                target[16 * f : 16 * f + 16, :] = jnp.concatenate([held[f, near, :], held[f, far, :]], axis=1)
            lanes = [
                hess[g, (far if z & 1 else near), 8 * (z >> 1) : 8 * (z >> 1) + 8] for z in range(4) for g in range(2)
            ]
            target[256:272, :] = jnp.concatenate(lanes + [jnp.zeros((16, 64), F32)], axis=1)
            target[272:336, :] = leaf_part[y]
            if y:
                encode_into(codes[y - 1], slab[...])


def histogram(feat_t, sketch, weight, leaf_part):
    cells = feat_t.shape[1]
    wide = 2 * BLOCK
    steps = cells // wide
    whole = pl.BlockSpec(memory_space=pltpu.VMEM)
    return pl.pallas_call(
        functools.partial(histogram_kernel, steps=steps),
        grid=(steps,),
        in_specs=[whole, pl.BlockSpec((32, wide), lambda j: (0, j)), whole, whole],
        out_specs=[whole] * 4,
        scratch_shapes=[pltpu.VMEM((16, 128, 64), F32), pltpu.VMEM((2, 128, 16), F32), pltpu.VMEM((336, 128), F32)],
        out_shape=[jax.ShapeDtypeStruct((336, 128), F32)]
        + [jax.ShapeDtypeStruct((encoded_rows(336), 128), jnp.int16)] * 3,
        compiler_params=pltpu.CompilerParams(vmem_limit_bytes=24 * 1024 * 1024),
        cost_estimate=pl.CostEstimate(flops=2 * 8192 * 4096 * 256, bytes_accessed=1500000, transcendentals=0),
        name="histogram",
    )(feat_t, sketch, weight, leaf_part)


def regroup_kernel(a, b, c, d, o0, o1, o2, o3):
    codes = (o1, o2, o3)
    total = a[...] + decode(b, 336) + decode(c, 336) + decode(d, 336)
    for z in range(4):
        lane = 64 * (z & 1) + 32 * (z >> 1)
        value = jnp.concatenate(
            [
                jnp.concatenate([total[64 * q : 64 * q + 64, lane : lane + 32] for q in range(4)], axis=1),
                jnp.concatenate([total[256:272, 16 * z : 16 * z + 16], jnp.zeros((16, 112), F32)], axis=1),
                total[272 + 8 * z : 280 + 8 * z, :],
                total[304 + 8 * z : 312 + 8 * z, :],
            ],
            axis=0,
        )
        if z:
            encode_into(codes[z - 1], value)
        else:
            o0[...] = value


def regroup(a, b, c, d):
    return pl.pallas_call(
        regroup_kernel,
        out_shape=[jax.ShapeDtypeStruct((96, 128), F32)]
        + [jax.ShapeDtypeStruct((encoded_rows(96), 128), jnp.int16)] * 3,
        compiler_params=pltpu.CompilerParams(vmem_limit_bytes=8 * 1024 * 1024),
        name="regroup",
    )(a, b, c, d)


def finish_kernel(a, b, c, d, grad_out, hess_out, leaf_out, rows, *, per_bin):
    total = a[...] + decode(b, 96) + decode(c, 96) + decode(d, 96)
    for q in range(4):
        rows[64 * q : 64 * q + 64, 0:32] = total[0:64, 32 * q : 32 * q + 32]
    for i in range(16):
        grad_out[i] = rows[pl.ds(i, 16, stride=16), :][:, 0:32]
    hess_out[...] = total[64:80, 0:16] / per_bin
    values = -total[80:88, :] / (total[88:96, :] + RIDGE)
    leaf_out[:, 0:128] = values[0:4]
    leaf_out[:, 128:256] = values[4:8]


def finish(a, b, c, d, per_bin):
    return pl.pallas_call(
        functools.partial(finish_kernel, per_bin=per_bin),
        out_shape=[
            jax.ShapeDtypeStruct((16, 16, 32), F32),
            jax.ShapeDtypeStruct((16, 16), F32),
            jax.ShapeDtypeStruct((4, 256), F32),
        ],
        scratch_shapes=[pltpu.VMEM((256, 128), F32)],
        compiler_params=pltpu.CompilerParams(vmem_limit_bytes=8 * 1024 * 1024),
        name="finish",
    )(a, b, c, d)


def swap(value, axis, flip):
    return lax.ppermute(value, axis, [(i, i ^ flip) for i in range(16)])


def pack(value):
    top = jnp.max(jnp.abs(value), axis=0, keepdims=True)
    exponent = jnp.ceil(jnp.log2(jnp.maximum(top, 1e-30)))
    return jnp.concatenate([value * jnp.exp2(-exponent), exponent], axis=0).astype(jnp.float16)


def unpack(code):
    whole = code.astype(F32)
    return whole[:-1] * jnp.exp2(whole[-1:])


def per_device(predictions, targets, row_weight, features, leaf, sketch_matrix):
    cells = predictions.shape[0]
    weight = row_weight.astype(F32).reshape(1, cells)
    args = (predictions, targets, weight, leaf.reshape(1, cells), sketch_matrix.T)
    other, leaf_part = gradient_half(*args, None, 4)
    arrived = swap(other, "out", 1)
    mine, leaf_part = gradient_half(*args, leaf_part, 0)
    chip = mine + arrived
    blocks = [chip[:, BLOCK * j : BLOCK * (j + 1)] for j in range(4)]
    far = [unpack(swap(pack(blocks[j]), "out", 2 * j)) for j in (2, 1, 3)]
    part = blocks[0] + far[0] + far[1] + far[2]
    own = (part + unpack(swap(pack(part), "out", 8))).astype(BF16)
    sketch = jnp.concatenate([own] + [swap(own, "out", 2 * j) for j in (1, 2, 3)], axis=1)
    sketch = jnp.concatenate([sketch, swap(sketch, "out", 1)], axis=1)
    slices = histogram(features.T, sketch, weight, leaf_part)
    slices = regroup(slices[0], *[swap(slices[j], "rows", j) for j in (1, 2, 3)])
    return tuple(
        finish(slices[0], *[swap(slices[j], "rows", 4 * j) for j in (1, 2, 3)], float(cells * 16 // BINS))
    )


def solution(mesh):
    return jax.shard_map(
        per_device,
        mesh=mesh,
        in_specs=(
            P("rows", "out"),
            P("rows", "out"),
            P("rows"),
            P("rows", "out"),
            P("rows"),
            P("out", None),
        ),
        out_specs=(P("rows", "out", None), P("rows", "out"), P("rows", "out")),
        check_vma=False,
    )
```

```python
import functools

import jax
import jax.numpy as jnp
from jax import lax
from jax.experimental import pallas as pl
from jax.experimental.pallas import tpu as pltpu
from jax.sharding import PartitionSpec as P

BINS = 256
LEAVES = 64
RIDGE = 1.0
F32 = jnp.float32
BF16 = jnp.bfloat16
BLOCK = 1024
CONTRACT_LAST = (((1,), (1,)), ((), ()))


def group_count(rows):
    return rows // 16


def encoded_rows(rows):
    return rows + -(-group_count(rows) // 16) * 16


def encode_into(out, value):
    rows = value.shape[0]
    count = group_count(rows)
    padded = encoded_rows(rows) - rows
    tops = [jnp.max(jnp.abs(value[16 * g : 16 * g + 16, :]), axis=0, keepdims=True) for g in range(count)]
    tops.append(jnp.zeros((padded - count, 128), F32))
    exponent = jnp.ceil(jnp.log2(jnp.maximum(jnp.concatenate(tops, axis=0), 1e-30)))
    scale = jnp.exp2(14.0 - exponent)
    for g in range(count):
        scaled = value[16 * g : 16 * g + 16, :] * scale[g : g + 1, :]
        out[16 * g : 16 * g + 16, :] = jnp.round(scaled).astype(jnp.int32).astype(jnp.int16)
    out[rows : rows + padded, :] = exponent.astype(jnp.int32).astype(jnp.int16)


def decode(code, rows):
    count = group_count(rows)
    whole = code[...].astype(jnp.int32).astype(F32)
    scale = jnp.exp2(whole[rows:, :] - 14.0)
    return jnp.concatenate([whole[16 * g : 16 * g + 16, :] * scale[g : g + 1, :] for g in range(count)], axis=0)


def cells_of(block):
    out_at = lax.axis_index("out")
    place = ((out_at & 1) ^ (block // 4)) * 4 + (((out_at >> 1) + block % 4) & 3)
    return pl.multiple_of(place * BLOCK, BLOCK)


def relative(value, size):
    rows_at = lax.axis_index("rows")
    return ((value - (rows_at >> 2) * (4 * size)) & (16 * size - 1)) ^ ((rows_at & 3) * size)


def gradient_kernel(*refs, first, parts):
    pred, targ, per_cell, matrix_t = refs[:4]
    leaf_in = refs[4] if len(refs) == 12 else None
    sketch_out, leaf_out, pred_here, targ_here, sums, weights = refs[-7:-1]
    arrived = refs[-1]
    size = BLOCK // parts
    copies = []
    for j in range(4):
        for part in range(parts):
            n = j * parts + part
            rows = pl.ds(pl.multiple_of(cells_of(j + first) + part * size, size), size)
            pair = [
                pltpu.make_async_copy(pred.at[rows, :], pred_here.at[n], arrived.at[0, n]),
                pltpu.make_async_copy(targ.at[rows, :], targ_here.at[n], arrived.at[1, n]),
            ]
            for copy in pair:
                copy.start()
            copies.append(pair)
    for j in range(4):
        lanes = pl.ds(cells_of(j + first), BLOCK)
        w_wide = per_cell[0:1, lanes]
        own = relative(per_cell[1:2, lanes].astype(jnp.int32), 4)
        place = ((own >> 2) & 3) * 16 + (own >> 4) * 4 + (own & 3)
        onehot = jnp.where(lax.broadcasted_iota(jnp.int32, (LEAVES, BLOCK), 0) == place, 1.0, 0.0).astype(BF16)
        w_cols = jnp.transpose(
            jnp.concatenate([w_wide[:, 128 * s : 128 * s + 128] for s in range(BLOCK // 128)], axis=0)
        )
        added = None
        for part in range(parts):
            n = j * parts + part
            for copy in copies[n]:
                copy.wait()
            pieces = []
            for s in range(size // 128):
                rows = slice(128 * s, 128 * s + 128)
                diff = pred_here[n, rows, :].astype(F32) - targ_here[n, rows, :].astype(F32)
                at = part * (size // 128) + s
                pieces.append((w_cols[:, at : at + 1] * diff).astype(BF16))
            gradient = jnp.concatenate(pieces, axis=0)
            sketch_out[:, n * size : n * size + size] = lax.dot_general(
                matrix_t[...], gradient, CONTRACT_LAST, preferred_element_type=F32
            )
            piece = jnp.dot(onehot[:, part * size : part * size + size], gradient, preferred_element_type=F32)
            added = piece if added is None else added + piece
        w_rows = jnp.broadcast_to(w_wide.astype(BF16), (16, BLOCK))
        w_added = lax.dot_general(onehot, w_rows, CONTRACT_LAST, preferred_element_type=F32)
        if j == 0:
            sums[...] = added
            weights[...] = w_added
        else:
            sums[...] += added
            weights[...] += w_added
    for y in range(4):
        for z in range(4):
            top = 16 * y + 4 * z
            pieces = [sums[top : top + 4, 0:128], sums[top : top + 4, 128:256]]
            pieces += [jnp.broadcast_to(weights[top : top + 4, 0:1], (4, 128))] * 2
            for value, at in zip(pieces, (8 * z, 8 * z + 4, 32 + 8 * z, 36 + 8 * z)):
                leaf_out[y, at : at + 4, :] = value if leaf_in is None else value + leaf_in[y, at : at + 4, :]


def gradient_half(pred, targ, per_cell, matrix_t, leaf_in, first):
    genes = pred.shape[1]
    half = pred.shape[0] // 2
    parts = 2
    given = [pred, targ, per_cell, matrix_t] + ([] if leaf_in is None else [leaf_in])
    whole = pl.BlockSpec(memory_space=pltpu.VMEM)
    return pl.pallas_call(
        functools.partial(gradient_kernel, first=first, parts=parts),
        in_specs=[pl.BlockSpec(memory_space=pltpu.HBM)] * 2 + [whole] * (len(given) - 2),
        out_specs=[whole, whole],
        scratch_shapes=[
            pltpu.VMEM((4 * parts, BLOCK // parts, genes), BF16),
            pltpu.VMEM((4 * parts, BLOCK // parts, genes), BF16),
            pltpu.VMEM((LEAVES, genes), F32),
            pltpu.VMEM((LEAVES, 16), F32),
            pltpu.SemaphoreType.DMA((2, 4 * parts)),
        ],
        out_shape=[
            jax.ShapeDtypeStruct((matrix_t.shape[0], half), F32),
            jax.ShapeDtypeStruct((4, 64, 128), F32),
        ],
        compiler_params=pltpu.CompilerParams(vmem_limit_bytes=51 * 1024 * 1024),
        cost_estimate=pl.CostEstimate(flops=2 * half * 256 * 300, bytes_accessed=5000000, transcendentals=0),
        name="gradient",
    )(*given)


def histogram_products(feat, sketch, per_cell, first):
    half = 4 * BLOCK
    places = [pl.ds(cells_of(first + b), BLOCK) for b in range(4)]
    sketch_all = sketch[...]
    w_row = jnp.concatenate([per_cell[0:1, place] for place in places], axis=1)
    w_all = jnp.broadcast_to(w_row.astype(BF16), (16, half))
    rows128 = lax.broadcasted_iota(jnp.int32, (128, half), 0).astype(BF16)
    rows16 = lax.broadcasted_iota(jnp.int32, (16, half), 0).astype(BF16)
    zero = jnp.zeros((), BF16)
    one = jnp.ones((), BF16)
    for f in range(16):
        own = relative(jnp.concatenate([feat[f : f + 1, place] for place in places], axis=1), 16)
        low = (own & 127).astype(F32).astype(BF16)
        top = own >> 7
        group = jnp.broadcast_to(top.astype(F32).astype(BF16), (32, half))
        left = jnp.where(rows128 == low, one, zero)
        spot = (top * 8 + (f % 8)).astype(F32).astype(BF16)
        right = jnp.concatenate(
            [
                jnp.where(group == zero, sketch_all, zero),
                jnp.where(group == zero, zero, sketch_all),
                jnp.where(rows16 == spot, w_all, zero),
            ],
            axis=0,
        )
        yield f, lax.dot_general(left, right, CONTRACT_LAST, preferred_element_type=F32)


def histogram_first_kernel(feat, sketch, per_cell, held, hess):
    for f, both in histogram_products(feat, sketch, per_cell, 0):
        held[f] = both[:, 0:64]
        if f % 8 == 0:
            hess[f // 8] = both[:, 64:80]
        else:
            hess[f // 8] += both[:, 64:80]


def histogram_second_kernel(feat, sketch, per_cell, held, hess_in, leaf_part, o0, o1, o2, o3, hess, s1, s2, s3):
    targets = (o0, s1, s2, s3)
    hess[...] = hess_in[...]
    for f, both in histogram_products(feat, sketch, per_cell, 4):
        total = held[f] + both[:, 0:64]
        for y in range(4):
            lanes = [total[16 * y : 16 * y + 16, :], total[64 + 16 * y : 80 + 16 * y, :]]
            targets[y][16 * f : 16 * f + 16, :] = jnp.concatenate(lanes, axis=1)
        hess[f // 8] += both[:, 64:80]
    for y in range(4):
        near, far = slice(16 * y, 16 * y + 16), slice(64 + 16 * y, 80 + 16 * y)
        lanes = [
            hess[g, (far if z & 1 else near), 8 * (z >> 1) : 8 * (z >> 1) + 8] for z in range(4) for g in range(2)
        ]
        targets[y][256:272, :] = jnp.concatenate(lanes + [jnp.zeros((16, 64), F32)], axis=1)
        targets[y][272:336, :] = leaf_part[y]
        if y:
            encode_into((o1, o2, o3)[y - 1], targets[y][...])


HISTOGRAM_OPTIONS = dict(
    compiler_params=pltpu.CompilerParams(vmem_limit_bytes=24 * 1024 * 1024),
    cost_estimate=pl.CostEstimate(flops=4096 * 4096 * 256, bytes_accessed=1500000, transcendentals=0),
)


def histogram_first(feat_t, sketch, per_cell):
    return pl.pallas_call(
        histogram_first_kernel,
        out_shape=[jax.ShapeDtypeStruct((16, 128, 64), F32), jax.ShapeDtypeStruct((2, 128, 16), F32)],
        name="histogram_first",
        **HISTOGRAM_OPTIONS,
    )(feat_t, sketch, per_cell)


def histogram_second(feat_t, sketch, per_cell, held, hess, leaf_part):
    return pl.pallas_call(
        histogram_second_kernel,
        scratch_shapes=[pltpu.VMEM((2, 128, 16), F32)] + [pltpu.VMEM((336, 128), F32)] * 3,
        out_shape=[jax.ShapeDtypeStruct((336, 128), F32)]
        + [jax.ShapeDtypeStruct((encoded_rows(336), 128), jnp.int16)] * 3,
        name="histogram_second",
        **HISTOGRAM_OPTIONS,
    )(feat_t, sketch, per_cell, held, hess, leaf_part)


def regroup_kernel(a, b, c, d, o0, o1, o2, o3):
    codes = (o1, o2, o3)
    total = a[...] + decode(b, 336) + decode(c, 336) + decode(d, 336)
    for z in range(4):
        lane = 64 * (z & 1) + 32 * (z >> 1)
        value = jnp.concatenate(
            [
                jnp.concatenate([total[64 * q : 64 * q + 64, lane : lane + 32] for q in range(4)], axis=1),
                jnp.concatenate([total[256:272, 16 * z : 16 * z + 16], jnp.zeros((16, 112), F32)], axis=1),
                total[272 + 8 * z : 280 + 8 * z, :],
                total[304 + 8 * z : 312 + 8 * z, :],
            ],
            axis=0,
        )
        if z:
            encode_into(codes[z - 1], value)
        else:
            o0[...] = value


def regroup(a, b, c, d):
    return pl.pallas_call(
        regroup_kernel,
        out_shape=[jax.ShapeDtypeStruct((96, 128), F32)]
        + [jax.ShapeDtypeStruct((encoded_rows(96), 128), jnp.int16)] * 3,
        compiler_params=pltpu.CompilerParams(vmem_limit_bytes=8 * 1024 * 1024),
        name="regroup",
    )(a, b, c, d)


def finish_kernel(a, b, c, d, grad_out, hess_out, leaf_out, rows, *, per_bin):
    total = a[...] + decode(b, 96) + decode(c, 96) + decode(d, 96)
    for q in range(4):
        rows[64 * q : 64 * q + 64, 0:32] = total[0:64, 32 * q : 32 * q + 32]
    for i in range(16):
        grad_out[i] = rows[pl.ds(i, 16, stride=16), :][:, 0:32]
    hess_out[...] = total[64:80, 0:16] / per_bin
    values = -total[80:88, :] / (total[88:96, :] + RIDGE)
    leaf_out[:, 0:128] = values[0:4]
    leaf_out[:, 128:256] = values[4:8]


def finish(a, b, c, d, per_bin):
    return pl.pallas_call(
        functools.partial(finish_kernel, per_bin=per_bin),
        out_shape=[
            jax.ShapeDtypeStruct((16, 16, 32), F32),
            jax.ShapeDtypeStruct((16, 16), F32),
            jax.ShapeDtypeStruct((4, 256), F32),
        ],
        scratch_shapes=[pltpu.VMEM((256, 128), F32)],
        compiler_params=pltpu.CompilerParams(vmem_limit_bytes=8 * 1024 * 1024),
        name="finish",
    )(a, b, c, d)


def swap(value, axis, flip):
    return lax.ppermute(value, axis, [(i, i ^ flip) for i in range(16)])


def shift(value, axis, unit, step):
    place = lambda i: (i // unit) % 4
    return lax.ppermute(
        value, axis, [(i, i + ((place(i) + step) % 4 - place(i)) * unit) for i in range(16)]
    )


def pack(value):
    top = jnp.max(jnp.abs(value), axis=0, keepdims=True)
    exponent = jnp.ceil(jnp.log2(jnp.maximum(top, 1e-30)))
    return jnp.concatenate([value * jnp.exp2(-exponent), exponent], axis=0).astype(jnp.float16)


def unpack(code):
    whole = code.astype(F32)
    return whole[:-1] * jnp.exp2(whole[-1:])


def per_device(predictions, targets, row_weight, features, leaf, sketch_matrix):
    cells = predictions.shape[0]
    per_cell = jnp.stack([row_weight.astype(F32), leaf.astype(F32)])
    features_t = features.T
    args = (predictions, targets, per_cell, sketch_matrix.T)
    other, leaf_part = gradient_half(*args, None, 4)
    arrived = swap(other, "out", 1)
    mine, leaf_part = gradient_half(*args, leaf_part, 0)
    chip = mine + arrived
    blocks = [chip[:, BLOCK * j : BLOCK * (j + 1)] for j in range(4)]
    far = [unpack(shift(pack(blocks[j]), "out", 2, j)) for j in (2, 1, 3)]
    part = blocks[0] + far[0] + far[1] + far[2]
    own = (part + unpack(swap(pack(part), "out", 8))).astype(BF16)
    near_half = jnp.concatenate([own] + [shift(own, "out", 2, -j) for j in (1, 2, 3)], axis=1)
    far_half = swap(near_half, "out", 1)
    held = histogram_first(features_t, near_half, per_cell)
    slices = histogram_second(features_t, far_half, per_cell, *held, leaf_part)
    slices = regroup(slices[0], *[swap(slices[j], "rows", j) for j in (1, 2, 3)])
    return tuple(
        finish(slices[0], *[shift(slices[j], "rows", 4, j) for j in (1, 2, 3)], float(cells * 16 // BINS))
    )


def solution(mesh):
    return jax.shard_map(
        per_device,
        mesh=mesh,
        in_specs=(
            P("rows", "out"),
            P("rows", "out"),
            P("rows"),
            P("rows", "out"),
            P("rows"),
            P("out", None),
        ),
        out_specs=(P("rows", "out", None), P("rows", "out"), P("rows", "out")),
        check_vma=False,
    )
```

```python
import functools

import jax
import jax.numpy as jnp
from jax import lax
from jax.experimental import pallas as pl
from jax.experimental.pallas import tpu as pltpu
from jax.sharding import PartitionSpec as P

BINS = 256
LEAVES = 64
RIDGE = 1.0
F32 = jnp.float32
BF16 = jnp.bfloat16
BLOCK = 1024
CONTRACT_LAST = (((1,), (1,)), ((), ()))


BIN_GROUPS = [32] * 8 + [16, 32]
OWN_GROUPS = [16] * 6


def encoded_rows(groups):
    return sum(groups) + 16


def starts_of(groups):
    return [sum(groups[:g]) for g in range(len(groups))]


def encode_into(out, value, groups):
    rows = sum(groups)
    tops = [
        jnp.max(jnp.abs(value[at : at + size, :]), axis=0, keepdims=True) for at, size in zip(starts_of(groups), groups)
    ]
    tops.append(jnp.zeros((16 - len(groups), 128), F32))
    exponent = jnp.ceil(jnp.log2(jnp.maximum(jnp.concatenate(tops, axis=0), 1e-30)))
    scale = jnp.exp2(14.0 - exponent)
    for g, (at, size) in enumerate(zip(starts_of(groups), groups)):
        scaled = value[at : at + size, :] * scale[g : g + 1, :]
        out[at : at + size, :] = jnp.round(scaled).astype(jnp.int32).astype(jnp.int16)
    out[rows : rows + 16, :] = exponent.astype(jnp.int32).astype(jnp.int16)


def decode(code, groups):
    whole = code[...].astype(jnp.int32).astype(F32)
    scale = jnp.exp2(whole[sum(groups) :, :] - 14.0)
    parts = [
        whole[at : at + size, :] * scale[g : g + 1, :] for g, (at, size) in enumerate(zip(starts_of(groups), groups))
    ]
    return jnp.concatenate(parts, axis=0)


def cells_place(block):
    return pl.multiple_of(cells_of(block) // 128, BLOCK // 128)


def one_row(tile):
    return jnp.concatenate([tile[r : r + 1, :] for r in range(tile.shape[0])], axis=1)


def cells_of(block):
    out_at = lax.axis_index("out")
    place = ((out_at & 1) ^ (block // 4)) * 4 + (((out_at >> 1) + block % 4) & 3)
    return pl.multiple_of(place * BLOCK, BLOCK)


def relative(value, size):
    rows_at = lax.axis_index("rows")
    return ((value - (rows_at >> 2) * (4 * size)) & (16 * size - 1)) ^ ((rows_at & 3) * size)


def gradient_kernel(
    pred, targ, weight_far, leaf_far, matrix_far, sketch_out, leaf_out,
    pred_here, targ_here, weight, leaf, matrix_t, sums, weights, weight_wide, arrived, small_arrived, *, blocks,
):
    small = [
        pltpu.make_async_copy(far, here, small_arrived.at[n])
        for n, (far, here) in enumerate([(weight_far, weight), (leaf_far, leaf), (matrix_far, matrix_t)])
    ]
    for copy in small:
        copy.start()
    copies = []
    for n, block in enumerate(blocks):
        rows = pl.ds(cells_of(block), BLOCK)
        pair = [
            pltpu.make_async_copy(pred.at[rows, :], pred_here.at[n], arrived.at[0, n]),
            pltpu.make_async_copy(targ.at[rows, :], targ_here.at[n], arrived.at[1, n]),
        ]
        for copy in pair:
            copy.start()
        copies.append(pair)
    for copy in small:
        copy.wait()
    weight_wide[...] = weight[...].astype(F32)
    for n, block in enumerate(blocks):
        tile = pl.ds(cells_place(block), BLOCK // 128)
        w_tile = weight_wide[tile, :]
        own = relative(one_row(leaf[tile, :]), 4)
        place = ((own >> 2) & 3) * 16 + (own >> 4) * 4 + (own & 3)
        onehot = jnp.where(lax.broadcasted_iota(jnp.int32, (LEAVES, BLOCK), 0) == place, 1.0, 0.0).astype(BF16)
        w_cols = jnp.transpose(w_tile)
        for copy in copies[n]:
            copy.wait()
        pieces = []
        for s in range(BLOCK // 128):
            rows = slice(128 * s, 128 * s + 128)
            diff = pred_here[n, rows, :].astype(F32) - targ_here[n, rows, :].astype(F32)
            pieces.append((w_cols[:, s : s + 1] * diff).astype(BF16))
        gradient = jnp.concatenate(pieces, axis=0)
        sketch_out[:, n * BLOCK : n * BLOCK + BLOCK] = lax.dot_general(
            matrix_t[...], gradient, CONTRACT_LAST, preferred_element_type=F32
        )
        added = jnp.dot(onehot, gradient, preferred_element_type=F32)
        w_rows = jnp.broadcast_to(one_row(w_tile).astype(BF16), (16, BLOCK))
        w_added = lax.dot_general(onehot, w_rows, CONTRACT_LAST, preferred_element_type=F32)
        if n == 0:
            sums[...] = added
            weights[...] = w_added
        else:
            sums[...] += added
            weights[...] += w_added
    for y in range(4):
        for z in range(4):
            top = 16 * y + 4 * z
            for h in range(2):
                at = 8 * z + 4 * h
                leaf_out[y, at : at + 4, :] = sums[top : top + 4, 128 * h : 128 * h + 128]
        leaf_out[y, 32:48, :] = jnp.broadcast_to(weights[16 * y : 16 * y + 16, 0:1], (16, 128))


def gradient(pred, targ, weight, leaf, matrix_t, blocks, room):
    genes = pred.shape[1]
    count = len(blocks)
    whole = pl.BlockSpec(memory_space=pltpu.VMEM)
    return pl.pallas_call(
        functools.partial(gradient_kernel, blocks=blocks),
        in_specs=[pl.BlockSpec(memory_space=pl.ANY)] * 5,
        out_specs=[whole, whole],
        scratch_shapes=[
            pltpu.VMEM((count, BLOCK, genes), BF16),
            pltpu.VMEM((count, BLOCK, genes), BF16),
            pltpu.VMEM(weight.shape, weight.dtype),
            pltpu.VMEM(leaf.shape, leaf.dtype),
            pltpu.VMEM(matrix_t.shape, matrix_t.dtype),
            pltpu.VMEM((LEAVES, genes), F32),
            pltpu.VMEM((LEAVES, 16), F32),
            pltpu.VMEM(weight.shape, F32),
            pltpu.SemaphoreType.DMA((2, count)),
            pltpu.SemaphoreType.DMA((3,)),
        ],
        out_shape=[
            jax.ShapeDtypeStruct((matrix_t.shape[0], count * BLOCK), F32),
            jax.ShapeDtypeStruct((4, 48, 128), F32),
        ],
        compiler_params=pltpu.CompilerParams(vmem_limit_bytes=room * 1024 * 1024),
        cost_estimate=pl.CostEstimate(flops=count * 500000000, bytes_accessed=count * 1500000, transcendentals=0),
        name="gradient",
    )(pred, targ, weight, leaf, matrix_t)


def histogram_products(feat, sketch, weight, weight_wide, blocks):
    wide = len(blocks) * BLOCK
    places = [pl.ds(cells_of(block), BLOCK) for block in blocks]
    sketch_all = sketch[...]
    weight_wide[...] = weight[...].astype(F32)
    tiles = [weight_wide[pl.ds(cells_place(block), BLOCK // 128), :] for block in blocks]
    w_row = jnp.concatenate([one_row(tile) for tile in tiles], axis=1)
    w_all = jnp.broadcast_to(w_row.astype(BF16), (16, wide))
    rows128 = lax.broadcasted_iota(jnp.int32, (128, wide), 0).astype(BF16)
    rows16 = lax.broadcasted_iota(jnp.int32, (16, wide), 0).astype(BF16)
    zero = jnp.zeros((), BF16)
    one = jnp.ones((), BF16)
    for f in range(16):
        own = relative(jnp.concatenate([feat[f : f + 1, place] for place in places], axis=1), 16)
        low = (own & 127).astype(F32).astype(BF16)
        top = own >> 7
        group = jnp.broadcast_to(top.astype(F32).astype(BF16), (32, wide))
        left = jnp.where(rows128 == low, one, zero)
        spot = (top * 8 + (f % 8)).astype(F32).astype(BF16)
        right = jnp.concatenate(
            [
                jnp.where(group == zero, sketch_all, zero),
                jnp.where(group == zero, zero, sketch_all),
                jnp.where(rows16 == spot, w_all, zero),
            ],
            axis=0,
        )
        yield f, lax.dot_general(left, right, CONTRACT_LAST, preferred_element_type=F32)


def histogram_part_kernel(feat, sketch, weight, *refs, blocks):
    held, hess, weight_wide = refs[-3:]
    before = refs[:-3]
    if before:
        hess[...] = before[1][...]
    for f, both in histogram_products(feat, sketch, weight, weight_wide, blocks):
        held[f] = both[:, 0:64] + before[0][f] if before else both[:, 0:64]
        if f % 8 == 0 and not before:
            hess[f // 8] = both[:, 64:80]
        else:
            hess[f // 8] += both[:, 64:80]


def histogram_last_kernel(
    feat, sketch, weight, held, hess_in, leaf_a, leaf_b, leaf_c, o0, o1, o2, o3, hess, s1, s2, s3, weight_wide, *, blocks
):
    targets = (o0, s1, s2, s3)
    hess[...] = hess_in[...]
    for f, both in histogram_products(feat, sketch, weight, weight_wide, blocks):
        total = held[f] + both[:, 0:64]
        for y in range(4):
            lanes = [total[16 * y : 16 * y + 16, :], total[64 + 16 * y : 80 + 16 * y, :]]
            targets[y][16 * f : 16 * f + 16, :] = jnp.concatenate(lanes, axis=1)
        hess[f // 8] += both[:, 64:80]
    for y in range(4):
        near, far = slice(16 * y, 16 * y + 16), slice(64 + 16 * y, 80 + 16 * y)
        lanes = [
            hess[g, (far if z & 1 else near), 8 * (z >> 1) : 8 * (z >> 1) + 8] for z in range(4) for g in range(2)
        ]
        leaf_part = leaf_a[y] + leaf_b[y] + leaf_c[y]
        targets[y][256:272, :] = jnp.concatenate(lanes + [leaf_part[32:48, 64:128]], axis=1)
        targets[y][272:304, :] = leaf_part[0:32, :]
        if y:
            encode_into((o1, o2, o3)[y - 1], targets[y][...], BIN_GROUPS)


def histogram_options(blocks):
    return dict(
        compiler_params=pltpu.CompilerParams(vmem_limit_bytes=24 * 1024 * 1024),
        cost_estimate=pl.CostEstimate(
            flops=len(blocks) * 1024 * 4096 * 256, bytes_accessed=len(blocks) * 300000, transcendentals=0
        ),
        name="histogram",
    )


def histogram_part(feat_t, sketch, weight, before, blocks):
    return pl.pallas_call(
        functools.partial(histogram_part_kernel, blocks=blocks),
        scratch_shapes=[pltpu.VMEM(weight.shape, F32)],
        out_shape=[jax.ShapeDtypeStruct((16, 128, 64), F32), jax.ShapeDtypeStruct((2, 128, 16), F32)],
        **histogram_options(blocks),
    )(feat_t, sketch, weight, *before)


def histogram_last(feat_t, sketch, weight, before, leaf_parts, blocks):
    return pl.pallas_call(
        functools.partial(histogram_last_kernel, blocks=blocks),
        scratch_shapes=[pltpu.VMEM((2, 128, 16), F32)] + [pltpu.VMEM((304, 128), F32)] * 3
        + [pltpu.VMEM(weight.shape, F32)],
        out_shape=[jax.ShapeDtypeStruct((304, 128), F32)]
        + [jax.ShapeDtypeStruct((encoded_rows(BIN_GROUPS), 128), jnp.int16)] * 3,
        **histogram_options(blocks),
    )(feat_t, sketch, weight, *before, *leaf_parts)


def regroup_kernel(a, b, c, d, o0, o1, o2, o3):
    codes = (o1, o2, o3)
    total = a[...] + decode(b, BIN_GROUPS) + decode(c, BIN_GROUPS) + decode(d, BIN_GROUPS)
    for z in range(4):
        lane = 64 * (z & 1) + 32 * (z >> 1)
        leaf_weights = jnp.concatenate([total[256 + 4 * z : 260 + 4 * z, 64:128]] * 4, axis=0)
        value = jnp.concatenate(
            [
                jnp.concatenate([total[64 * q : 64 * q + 64, lane : lane + 32] for q in range(4)], axis=1),
                jnp.concatenate(
                    [total[256:272, 16 * z : 16 * z + 16], jnp.zeros((16, 48), F32), leaf_weights], axis=1
                ),
                total[272 + 8 * z : 280 + 8 * z, :],
                jnp.zeros((8, 128), F32),
            ],
            axis=0,
        )
        if z:
            encode_into(codes[z - 1], value, OWN_GROUPS)
        else:
            o0[...] = value


def regroup(a, b, c, d):
    return pl.pallas_call(
        regroup_kernel,
        out_shape=[jax.ShapeDtypeStruct((96, 128), F32)]
        + [jax.ShapeDtypeStruct((encoded_rows(OWN_GROUPS), 128), jnp.int16)] * 3,
        compiler_params=pltpu.CompilerParams(vmem_limit_bytes=8 * 1024 * 1024),
        name="regroup",
    )(a, b, c, d)


def finish_kernel(a, b, c, d, grad_out, hess_out, leaf_out, rows, *, per_bin):
    total = a[...] + decode(b, OWN_GROUPS) + decode(c, OWN_GROUPS) + decode(d, OWN_GROUPS)
    for q in range(4):
        rows[64 * q : 64 * q + 64, 0:32] = total[0:64, 32 * q : 32 * q + 32]
    for i in range(16):
        grad_out[i] = rows[pl.ds(i, 16, stride=16), :][:, 0:32]
    hess_out[...] = total[64:80, 0:16] / per_bin
    values = -total[80:88, :] / (total[64:72, 64:65] + RIDGE)
    leaf_out[:, 0:128] = values[0:4]
    leaf_out[:, 128:256] = values[4:8]


def finish(a, b, c, d, per_bin):
    return pl.pallas_call(
        functools.partial(finish_kernel, per_bin=per_bin),
        out_shape=[
            jax.ShapeDtypeStruct((16, 16, 32), F32),
            jax.ShapeDtypeStruct((16, 16), F32),
            jax.ShapeDtypeStruct((4, 256), F32),
        ],
        scratch_shapes=[pltpu.VMEM((256, 128), F32)],
        compiler_params=pltpu.CompilerParams(vmem_limit_bytes=8 * 1024 * 1024),
        name="finish",
    )(a, b, c, d)


def swap(value, axis, flip):
    return lax.ppermute(value, axis, [(i, i ^ flip) for i in range(16)])


def shift(value, axis, unit, step):
    place = lambda i: (i // unit) % 4
    return lax.ppermute(
        value, axis, [(i, i + ((place(i) + step) % 4 - place(i)) * unit) for i in range(16)]
    )


def pack(value):
    top = jnp.max(jnp.abs(value), axis=0, keepdims=True)
    exponent = jnp.ceil(jnp.log2(jnp.maximum(top, 1e-30)))
    return jnp.concatenate([value * jnp.exp2(-exponent), exponent], axis=0).astype(jnp.float16)


def unpack(code):
    whole = code.astype(F32)
    return whole[:-1] * jnp.exp2(whole[-1:])


def per_device(predictions, targets, row_weight, features, leaf, sketch_matrix):
    cells = predictions.shape[0]
    weight = row_weight.reshape(cells // 128, 128)
    features_t = features.T
    args = (predictions, targets, weight, leaf.reshape(cells // 128, 128), sketch_matrix.T)
    other, leaf_a = gradient(*args, [5, 6, 7, 4], 58)
    arrived = swap(other, "out", 1)
    mine, leaf_b = gradient(*args, [1, 2, 3], 51)
    chip = mine + arrived[:, : 3 * BLOCK]
    codes = [pack(chip[:, BLOCK * (j - 1) : BLOCK * j]) for j in (2, 1, 3)]
    codes, matrix_t = lax.optimization_barrier((codes, args[-1]))
    far = [unpack(shift(code, "out", 2, j)) for code, j in zip(codes, (2, 1, 3))]
    last, leaf_c = gradient(*args[:-1], matrix_t, [0], 51)
    part = last + arrived[:, 3 * BLOCK :] + far[0] + far[1] + far[2]
    own = (part + unpack(swap(pack(part), "out", 8))).astype(BF16)
    held = histogram_part(features_t, own, weight, [], [0])
    near = jnp.concatenate([shift(own, "out", 2, -j) for j in (1, 2, 3)], axis=1)
    across = swap(jnp.concatenate([own, near], axis=1), "out", 1)
    held = histogram_part(features_t, near, weight, held, [1, 2, 3])
    slices = histogram_last(features_t, across, weight, held, (leaf_a, leaf_b, leaf_c), [4, 5, 6, 7])
    slices = regroup(slices[0], *[swap(slices[j], "rows", j) for j in (1, 2, 3)])
    return tuple(
        finish(slices[0], *[shift(slices[j], "rows", 4, j) for j in (1, 2, 3)], float(cells * 16 // BINS))
    )


def solution(mesh):
    return jax.shard_map(
        per_device,
        mesh=mesh,
        in_specs=(
            P("rows", "out"),
            P("rows", "out"),
            P("rows"),
            P("rows", "out"),
            P("rows"),
            P("out", None),
        ),
        out_specs=(P("rows", "out", None), P("rows", "out"), P("rows", "out")),
        check_vma=False,
    )
```

```python
import functools

import jax
import jax.numpy as jnp
from jax import lax
from jax.experimental import pallas as pl
from jax.experimental.pallas import tpu as pltpu
from jax.sharding import PartitionSpec as P

BINS = 256
LEAVES = 64
RIDGE = 1.0
F32 = jnp.float32
BF16 = jnp.bfloat16
BLOCK = 1024
CONTRACT_LAST = (((1,), (1,)), ((), ()))


BIN_GROUPS = [32] * 8 + [16, 32]
OWN_GROUPS = [16] * 6


def encoded_rows(groups):
    return sum(groups) + 16


def starts_of(groups):
    return [sum(groups[:g]) for g in range(len(groups))]


def encode_into(out, value, groups):
    rows = sum(groups)
    tops = [
        jnp.max(jnp.abs(value[at : at + size, :]), axis=0, keepdims=True) for at, size in zip(starts_of(groups), groups)
    ]
    tops.append(jnp.zeros((16 - len(groups), 128), F32))
    exponent = jnp.ceil(jnp.log2(jnp.maximum(jnp.concatenate(tops, axis=0), 1e-30)))
    scale = jnp.exp2(14.0 - exponent)
    for g, (at, size) in enumerate(zip(starts_of(groups), groups)):
        scaled = value[at : at + size, :] * scale[g : g + 1, :]
        out[at : at + size, :] = jnp.round(scaled).astype(jnp.int32).astype(jnp.int16)
    out[rows : rows + 16, :] = exponent.astype(jnp.int32).astype(jnp.int16)


def decode(code, groups):
    whole = code[...].astype(jnp.int32).astype(F32)
    scale = jnp.exp2(whole[sum(groups) :, :] - 14.0)
    parts = [
        whole[at : at + size, :] * scale[g : g + 1, :] for g, (at, size) in enumerate(zip(starts_of(groups), groups))
    ]
    return jnp.concatenate(parts, axis=0)


def cells_place(block):
    return pl.multiple_of(cells_of(block) // 128, BLOCK // 128)


def one_row(tile):
    return jnp.concatenate([tile[r : r + 1, :] for r in range(tile.shape[0])], axis=1)


def cells_of(block):
    out_at = lax.axis_index("out")
    place = ((out_at & 1) ^ (block // 4)) * 4 + (((out_at >> 1) + block % 4) & 3)
    return pl.multiple_of(place * BLOCK, BLOCK)


def relative(value, size):
    rows_at = lax.axis_index("rows")
    return ((value - (rows_at >> 2) * (4 * size)) & (16 * size - 1)) ^ ((rows_at & 3) * size)


def gradient_kernel(
    pred, targ, weight_far, leaf_far, matrix_far, sketch_out, leaf_out,
    pred_here, targ_here, weight, leaf, matrix_t, sums, weights, weight_wide, arrived, small_arrived, *, blocks,
):
    depth = 2 if len(blocks) == 4 else 3
    small = [
        pltpu.make_async_copy(far, here, small_arrived.at[n])
        for n, (far, here) in enumerate([(weight_far, weight), (leaf_far, leaf), (matrix_far, matrix_t)])
    ]
    for copy in small:
        copy.start()
    copies = []
    for n, block in enumerate(blocks):
        rows = pl.ds(cells_of(block), BLOCK)
        pair = [
            pltpu.make_async_copy(pred.at[rows, :], pred_here.at[n], arrived.at[0, n]),
            pltpu.make_async_copy(targ.at[rows, :], targ_here.at[n], arrived.at[1, n]),
        ]
        copies.append(pair)
    for pair in copies[:depth]:
        for copy in pair:
            copy.start()
    for copy in small:
        copy.wait()
    weight_wide[...] = weight[...].astype(F32)
    for n, block in enumerate(blocks):
        tile = pl.ds(cells_place(block), BLOCK // 128)
        w_tile = weight_wide[tile, :]
        own = relative(one_row(leaf[tile, :]), 4)
        place = ((own >> 2) & 3) * 16 + (own >> 4) * 4 + (own & 3)
        onehot = jnp.where(lax.broadcasted_iota(jnp.int32, (LEAVES, BLOCK), 0) == place, 1.0, 0.0).astype(BF16)
        w_cols = jnp.transpose(w_tile)
        for copy in copies[n]:
            copy.wait()
        for copy in copies[n + depth] if n + depth < len(blocks) else []:
            copy.start()
        pieces = []
        for s in range(BLOCK // 128):
            rows = slice(128 * s, 128 * s + 128)
            diff = pred_here[n, rows, :].astype(F32) - targ_here[n, rows, :].astype(F32)
            pieces.append((w_cols[:, s : s + 1] * diff).astype(BF16))
        gradient = jnp.concatenate(pieces, axis=0)
        sketch_out[:, n * BLOCK : n * BLOCK + BLOCK] = lax.dot_general(
            matrix_t[...], gradient, CONTRACT_LAST, preferred_element_type=F32
        )
        added = jnp.dot(onehot, gradient, preferred_element_type=F32)
        w_rows = jnp.broadcast_to(one_row(w_tile).astype(BF16), (16, BLOCK))
        w_added = lax.dot_general(onehot, w_rows, CONTRACT_LAST, preferred_element_type=F32)
        if n == 0:
            sums[...] = added
            weights[...] = w_added
        else:
            sums[...] += added
            weights[...] += w_added
    for y in range(4):
        for z in range(4):
            top = 16 * y + 4 * z
            for h in range(2):
                at = 8 * z + 4 * h
                leaf_out[y, at : at + 4, :] = sums[top : top + 4, 128 * h : 128 * h + 128]
        leaf_out[y, 32:48, :] = jnp.broadcast_to(weights[16 * y : 16 * y + 16, 0:1], (16, 128))


def gradient(pred, targ, weight, leaf, matrix_t, blocks, room):
    genes = pred.shape[1]
    count = len(blocks)
    whole = pl.BlockSpec(memory_space=pltpu.VMEM)
    return pl.pallas_call(
        functools.partial(gradient_kernel, blocks=blocks),
        in_specs=[pl.BlockSpec(memory_space=pl.ANY)] * 5,
        out_specs=[whole, whole],
        scratch_shapes=[
            pltpu.VMEM((count, BLOCK, genes), BF16),
            pltpu.VMEM((count, BLOCK, genes), BF16),
            pltpu.VMEM(weight.shape, weight.dtype),
            pltpu.VMEM(leaf.shape, leaf.dtype),
            pltpu.VMEM(matrix_t.shape, matrix_t.dtype),
            pltpu.VMEM((LEAVES, genes), F32),
            pltpu.VMEM((LEAVES, 16), F32),
            pltpu.VMEM(weight.shape, F32),
            pltpu.SemaphoreType.DMA((2, count)),
            pltpu.SemaphoreType.DMA((3,)),
        ],
        out_shape=[
            jax.ShapeDtypeStruct((matrix_t.shape[0], count * BLOCK), F32),
            jax.ShapeDtypeStruct((4, 48, 128), F32),
        ],
        compiler_params=pltpu.CompilerParams(vmem_limit_bytes=room * 1024 * 1024),
        cost_estimate=pl.CostEstimate(flops=count * 500000000, bytes_accessed=count * 1500000, transcendentals=0),
        name="gradient",
    )(pred, targ, weight, leaf, matrix_t)


def histogram_products(feat, sketch, weight, weight_wide, blocks):
    wide = len(blocks) * BLOCK
    places = [pl.ds(cells_of(block), BLOCK) for block in blocks]
    sketch_all = sketch[...]
    weight_wide[...] = weight[...].astype(F32)
    tiles = [weight_wide[pl.ds(cells_place(block), BLOCK // 128), :] for block in blocks]
    w_row = jnp.concatenate([one_row(tile) for tile in tiles], axis=1)
    w_all = jnp.broadcast_to(w_row.astype(BF16), (16, wide))
    rows128 = lax.broadcasted_iota(jnp.int32, (128, wide), 0).astype(BF16)
    rows16 = lax.broadcasted_iota(jnp.int32, (16, wide), 0).astype(BF16)
    zero = jnp.zeros((), BF16)
    one = jnp.ones((), BF16)
    for f in range(16):
        own = relative(jnp.concatenate([feat[f : f + 1, place] for place in places], axis=1), 16)
        low = (own & 127).astype(F32).astype(BF16)
        top = own >> 7
        group = jnp.broadcast_to(top.astype(F32).astype(BF16), (32, wide))
        left = jnp.where(rows128 == low, one, zero)
        spot = (top * 8 + (f % 8)).astype(F32).astype(BF16)
        right = jnp.concatenate(
            [
                jnp.where(group == zero, sketch_all, zero),
                jnp.where(group == zero, zero, sketch_all),
                jnp.where(rows16 == spot, w_all, zero),
            ],
            axis=0,
        )
        yield f, lax.dot_general(left, right, CONTRACT_LAST, preferred_element_type=F32)


def histogram_part_kernel(feat, sketch, weight, *refs, blocks):
    held, hess, weight_wide = refs[-3:]
    before = refs[:-3]
    if before:
        hess[...] = before[1][...]
    for f, both in histogram_products(feat, sketch, weight, weight_wide, blocks):
        held[f] = both[:, 0:64] + before[0][f] if before else both[:, 0:64]
        if f % 8 == 0 and not before:
            hess[f // 8] = both[:, 64:80]
        else:
            hess[f // 8] += both[:, 64:80]


def histogram_last_kernel(
    feat, sketch, weight, held, hess_in, leaf_a, leaf_b, leaf_c, o0, o1, o2, o3, hess, s1, s2, s3, weight_wide, *, blocks
):
    targets = (o0, s1, s2, s3)
    hess[...] = hess_in[...]
    for f, both in histogram_products(feat, sketch, weight, weight_wide, blocks):
        total = held[f] + both[:, 0:64]
        for y in range(4):
            lanes = [total[16 * y : 16 * y + 16, :], total[64 + 16 * y : 80 + 16 * y, :]]
            targets[y][16 * f : 16 * f + 16, :] = jnp.concatenate(lanes, axis=1)
        hess[f // 8] += both[:, 64:80]
    for y in range(4):
        near, far = slice(16 * y, 16 * y + 16), slice(64 + 16 * y, 80 + 16 * y)
        lanes = [
            hess[g, (far if z & 1 else near), 8 * (z >> 1) : 8 * (z >> 1) + 8] for z in range(4) for g in range(2)
        ]
        leaf_part = leaf_a[y] + leaf_b[y] + leaf_c[y]
        targets[y][256:272, :] = jnp.concatenate(lanes + [leaf_part[32:48, 64:128]], axis=1)
        targets[y][272:304, :] = leaf_part[0:32, :]
        if y:
            encode_into((o1, o2, o3)[y - 1], targets[y][...], BIN_GROUPS)


def histogram_options(blocks):
    return dict(
        compiler_params=pltpu.CompilerParams(vmem_limit_bytes=24 * 1024 * 1024),
        cost_estimate=pl.CostEstimate(
            flops=len(blocks) * 1024 * 4096 * 256, bytes_accessed=len(blocks) * 300000, transcendentals=0
        ),
        name="histogram",
    )


def histogram_part(feat_t, sketch, weight, before, blocks):
    return pl.pallas_call(
        functools.partial(histogram_part_kernel, blocks=blocks),
        scratch_shapes=[pltpu.VMEM(weight.shape, F32)],
        out_shape=[jax.ShapeDtypeStruct((16, 128, 64), F32), jax.ShapeDtypeStruct((2, 128, 16), F32)],
        **histogram_options(blocks),
    )(feat_t, sketch, weight, *before)


def histogram_last(feat_t, sketch, weight, before, leaf_parts, blocks):
    return pl.pallas_call(
        functools.partial(histogram_last_kernel, blocks=blocks),
        scratch_shapes=[pltpu.VMEM((2, 128, 16), F32)] + [pltpu.VMEM((304, 128), F32)] * 3
        + [pltpu.VMEM(weight.shape, F32)],
        out_shape=[jax.ShapeDtypeStruct((304, 128), F32)]
        + [jax.ShapeDtypeStruct((encoded_rows(BIN_GROUPS), 128), jnp.int16)] * 3,
        **histogram_options(blocks),
    )(feat_t, sketch, weight, *before, *leaf_parts)


def regroup_kernel(a, b, c, d, o0, o1, o2, o3):
    codes = (o1, o2, o3)
    total = a[...] + decode(b, BIN_GROUPS) + decode(c, BIN_GROUPS) + decode(d, BIN_GROUPS)
    for z in range(4):
        lane = 64 * (z & 1) + 32 * (z >> 1)
        leaf_weights = jnp.concatenate([total[256 + 4 * z : 260 + 4 * z, 64:128]] * 4, axis=0)
        value = jnp.concatenate(
            [
                jnp.concatenate([total[64 * q : 64 * q + 64, lane : lane + 32] for q in range(4)], axis=1),
                jnp.concatenate(
                    [total[256:272, 16 * z : 16 * z + 16], jnp.zeros((16, 48), F32), leaf_weights], axis=1
                ),
                total[272 + 8 * z : 280 + 8 * z, :],
                jnp.zeros((8, 128), F32),
            ],
            axis=0,
        )
        if z:
            encode_into(codes[z - 1], value, OWN_GROUPS)
        else:
            o0[...] = value


def regroup(a, b, c, d):
    return pl.pallas_call(
        regroup_kernel,
        out_shape=[jax.ShapeDtypeStruct((96, 128), F32)]
        + [jax.ShapeDtypeStruct((encoded_rows(OWN_GROUPS), 128), jnp.int16)] * 3,
        compiler_params=pltpu.CompilerParams(vmem_limit_bytes=8 * 1024 * 1024),
        name="regroup",
    )(a, b, c, d)


def finish_kernel(a, b, c, d, grad_out, hess_out, leaf_out, rows, *, per_bin):
    total = a[...] + decode(b, OWN_GROUPS) + decode(c, OWN_GROUPS) + decode(d, OWN_GROUPS)
    for q in range(4):
        rows[64 * q : 64 * q + 64, 0:32] = total[0:64, 32 * q : 32 * q + 32]
    for i in range(16):
        grad_out[i] = rows[pl.ds(i, 16, stride=16), :][:, 0:32]
    hess_out[...] = total[64:80, 0:16] / per_bin
    values = -total[80:88, :] / (total[64:72, 64:65] + RIDGE)
    leaf_out[:, 0:128] = values[0:4]
    leaf_out[:, 128:256] = values[4:8]


def finish(a, b, c, d, per_bin):
    return pl.pallas_call(
        functools.partial(finish_kernel, per_bin=per_bin),
        out_shape=[
            jax.ShapeDtypeStruct((16, 16, 32), F32),
            jax.ShapeDtypeStruct((16, 16), F32),
            jax.ShapeDtypeStruct((4, 256), F32),
        ],
        scratch_shapes=[pltpu.VMEM((256, 128), F32)],
        compiler_params=pltpu.CompilerParams(vmem_limit_bytes=8 * 1024 * 1024),
        name="finish",
    )(a, b, c, d)


def swap(value, axis, flip):
    return lax.ppermute(value, axis, [(i, i ^ flip) for i in range(16)])


def shift(value, axis, unit, step):
    place = lambda i: (i // unit) % 4
    return lax.ppermute(
        value, axis, [(i, i + ((place(i) + step) % 4 - place(i)) * unit) for i in range(16)]
    )


def pack(value):
    top = jnp.max(jnp.abs(value), axis=0, keepdims=True)
    exponent = jnp.ceil(jnp.log2(jnp.maximum(top, 1e-30)))
    return jnp.concatenate([value * jnp.exp2(-exponent), exponent], axis=0).astype(jnp.float16)


def unpack(code):
    whole = code.astype(F32)
    return whole[:-1] * jnp.exp2(whole[-1:])


def per_device(predictions, targets, row_weight, features, leaf, sketch_matrix):
    cells = predictions.shape[0]
    weight = row_weight.reshape(cells // 128, 128)
    features_t = features.T
    args = (predictions, targets, weight, leaf.reshape(cells // 128, 128), sketch_matrix.T)
    other, leaf_a = gradient(*args, [5, 6, 7, 4], 58)
    arrived = swap(other, "out", 1)
    mine, leaf_b = gradient(*args, [1, 2, 3], 51)
    chip = mine + arrived[:, : 3 * BLOCK]
    codes = [pack(chip[:, BLOCK * (j - 1) : BLOCK * j]) for j in (2, 1, 3)]
    codes, matrix_t = lax.optimization_barrier((codes, args[-1]))
    far = [unpack(shift(code, "out", 2, j)) for code, j in zip(codes, (2, 1, 3))]
    last, leaf_c = gradient(*args[:-1], matrix_t, [0], 51)
    part = last + arrived[:, 3 * BLOCK :] + far[0] + far[1] + far[2]
    own = (part + unpack(swap(pack(part), "out", 8))).astype(BF16)
    held = histogram_part(features_t, own, weight, [], [0])
    near = jnp.concatenate([shift(own, "out", 2, -j) for j in (1, 2, 3)], axis=1)
    across = swap(jnp.concatenate([own, near], axis=1), "out", 1)
    held = histogram_part(features_t, near, weight, held, [1, 2, 3])
    slices = histogram_last(features_t, across, weight, held, (leaf_a, leaf_b, leaf_c), [4, 5, 6, 7])
    slices = regroup(slices[0], *[swap(slices[j], "rows", j) for j in (3, 2, 1)])
    return tuple(
        finish(slices[0], *[shift(slices[j], "rows", 4, j) for j in (1, 2, 3)], float(cells * 16 // BINS))
    )


def solution(mesh):
    return jax.shard_map(
        per_device,
        mesh=mesh,
        in_specs=(
            P("rows", "out"),
            P("rows", "out"),
            P("rows"),
            P("rows", "out"),
            P("rows"),
            P("out", None),
        ),
        out_specs=(P("rows", "out", None), P("rows", "out"), P("rows", "out")),
        check_vma=False,
    )
```
